32 devices in a mesh: comp: 2 (over y), ty: 4 (over z), tx: 4 (over x, core).
Axes of the slice: x: 2, y: 2, z: 4, core: 2. Of those that a mesh axis runs over, the one named last changes fastest.
Arguments:
- ocean: float32 [3, 64, 1024], P(None, 'ty', 'tx'), may hold values from -4 to 4
- tracers: float32 [19, 4, 16, 1024], P(None, 'ty', 'comp', 'tx'), may hold values from 0.05 to 3
- bottom: int32 [64, 16], P('ty', 'tx'), may hold values from 0 to 64, as said below
- stoich: float32 [14], replicated, may hold values from -3 to 3
Outputs:
- ocean_out: float32 [3, 64, 1024], P(None, 'ty', 'tx')
- tracers_out: float32 [19, 4, 16, 1024], P(None, 'ty', 'comp', 'tx')
The draws below stay inside these ranges and needn't reach their ends.
Inputs may be any that keep to these rules, and one draw needn't show every extreme that they name: bottom counts wet levels from the surface; 0 marks land, 64 a full column.
All inputs are finite; a program needn't handle non-finite values.
Results may differ from the reference program's by a relative error of at most 0.0003.
Values sent between devices are 32-bit elements; how exact they have to be, the bound alone decides.
A program may use at most 64 MiB of HBM per device.

```python
import math
import jax
import jax.numpy as jnp
from jax import lax

NTR = 19
LEV = 64
STEPS = 2
BANDS = 4
BAND = 16
NY = 64
NX = 16


def draw_bottom(key, part):
    raw_levels = jax.random.randint(key, (NY, NX), -16, LEV + 16)
    return jnp.clip(raw_levels, 0, LEV).astype(jnp.int32)


def steps_of(stream_key, dims, split, least, largest):
    loudness = 1.0
    for dim, parts in split:
        steps = jax.random.uniform(jax.random.fold_in(jax.random.fold_in(stream_key, 6), dim), (parts,), jnp.float32, least / len(split), largest / len(split))
        loudness = loudness * jnp.repeat(jnp.exp(steps), dims[dim] // parts).reshape((-1,) + (1,) * (len(dims) - 1 - dim))
    return loudness


def noise(rng, dims, deviation, bound, pieces=(), dtype=jnp.bfloat16):
    gain = steps_of(rng, dims, pieces, -0.22, 0.18) if pieces else 1.0
    entries = jax.random.normal(rng, dims, jnp.float32) * deviation * gain
    return jnp.minimum(jnp.maximum(entries, -bound), bound).astype(dtype)


def setup_inputs(seed: int = 0) -> dict:
    keys = jax.random.split(jax.random.key(seed), 5)
    return {
        "ocean": noise(keys[0], (3, NY, NX * LEV), 1.0, 4.0, ((1, 4), (2, 4)), jnp.float32),
        "tracers": jnp.clip(jnp.exp(math.log(3.0) - 4.0943445 * jax.random.uniform(keys[1], (NTR, BANDS, BAND, NX * LEV), jnp.float32) ** steps_of(keys[1], (NTR, BANDS, BAND, NX * LEV), ((1, 4), (2, 2), (3, 4)), -0.2, 0.2)), 0.05, 3.0),
        "bottom": draw_bottom(jax.random.fold_in(keys[4], 71), 0),
        "stoich": noise(keys[3], (NTR - 5,), 1.0, 3.0, (), jnp.float32),
    }


ATTEN_WATER = 0.04
ATTEN_CHL = 0.03
PRESSURE = 0.05
TIME_STEP = 0.2
CORIOLIS = 1.0
DAMPING = 0.05
HEAT_GAIN = 2.0
DIFFUSE = 0.2
ADVECT = 0.08
GROWTH = 1.0
HALF_LIGHT = 0.2
HALF_NUTRIENT = 0.5
TEMP_COEF = 0.1
GRAZE = 0.8
HALF_PREY = 0.3
MORTAL = 0.1
REMIN = 0.2
CHL_RELAX = 0.3
CHL_RATIO = 0.5
CHL_GAIN = 0.2
ASSIM = 0.3
GRAZER_LOSS = 0.05
REACT_STEP = 0.2


def level_sums(values, inclusive):
    count = values.shape[-1]
    level_ids = jnp.arange(count)
    if inclusive:
        ladder = level_ids[:, None] <= level_ids[None, :]
    else:
        ladder = level_ids[:, None] < level_ids[None, :]
    return jnp.dot(values, ladder.astype(jnp.float32), precision=lax.Precision.HIGHEST)


def optics(chloro, wet_mask):
    absorb = (ATTEN_WATER + ATTEN_CHL * jnp.maximum(chloro, 0.0)) * wet_mask
    sunlight = jnp.exp(-level_sums(absorb, False))
    heating = sunlight * (1.0 - jnp.exp(-absorb)) * wet_mask
    return sunlight, heating


def ocean_update(current, row_margin, column_margin, heating, wet_mask):
    east = current[0]
    north = current[1]
    temper = current[2]
    press_rows = PRESSURE * level_sums(row_margin, True)
    press_cols = PRESSURE * level_sums(column_margin, True)
    slope_x = 0.5 * (press_cols[:, 2:] - press_cols[:, :-2])
    slope_y = 0.5 * (press_rows[2:] - press_rows[:-2])
    spread = row_margin[2:] + row_margin[:-2] + column_margin[:, 2:] + column_margin[:, :-2] - 4.0 * temper
    new_east = wet_mask * ((1.0 - DAMPING) * east + TIME_STEP * (CORIOLIS * north - slope_x))
    new_north = wet_mask * ((1.0 - DAMPING) * north - TIME_STEP * (CORIOLIS * east + slope_y))
    new_temp = wet_mask * (temper + TIME_STEP * (HEAT_GAIN * heating + DIFFUSE * spread))
    return jnp.stack([new_east, new_north, new_temp])


def minmod(first, second):
    return jnp.where(first * second > 0.0, jnp.sign(first) * jnp.minimum(jnp.abs(first), jnp.abs(second)), 0.0)


def face_transport(field_wide, speed_wide, wet_wide, along_dim, cell_count):
    def window(values, offset):
        return lax.slice_in_dim(values, offset, offset + cell_count + 1, axis=along_dim)

    far_left = window(field_wide, 0)
    left_cell = window(field_wide, 1)
    right_cell = window(field_wide, 2)
    far_right = window(field_wide, 3)
    speed = 0.5 * (window(speed_wide, 1) + window(speed_wide, 2)) * window(wet_wide, 1) * window(wet_wide, 2)
    from_left = left_cell + 0.5 * minmod(left_cell - far_left, right_cell - left_cell)
    from_right = right_cell - 0.5 * minmod(right_cell - left_cell, far_right - right_cell)
    flux = ADVECT * speed * jnp.where(speed > 0.0, from_left, from_right)
    return lax.slice_in_dim(flux, 1, cell_count + 1, axis=along_dim) - lax.slice_in_dim(flux, 0, cell_count, axis=along_dim)


def reactions(advected, sunlight, temper, stoich, wet_mask):
    nutrient = jnp.maximum(advected[0], 0.0)
    phyto = jnp.maximum(advected[1], 0.0)
    chloro = jnp.maximum(advected[2], 0.0)
    grazer = jnp.maximum(advected[3], 0.0)
    detritus = jnp.maximum(advected[4], 0.0)
    uptake = GROWTH * sunlight / (sunlight + HALF_LIGHT) * nutrient / (nutrient + HALF_NUTRIENT) * jnp.exp(TEMP_COEF * temper)
    growth = uptake * phyto
    grazing = GRAZE * grazer * phyto * phyto / (phyto * phyto + HALF_PREY)
    dying = MORTAL * phyto
    remineral = REMIN * detritus
    core = jnp.stack([
        remineral - growth,
        growth - grazing - dying,
        CHL_RELAX * (CHL_RATIO * phyto - chloro) + CHL_GAIN * growth,
        ASSIM * grazing - GRAZER_LOSS * grazer,
        dying + (1.0 - ASSIM) * grazing + GRAZER_LOSS * grazer - remineral,
    ])
    others = stoich.reshape((stoich.shape[0],) + (1,) * growth.ndim) * (growth - remineral)[None]
    change_all = jnp.concatenate([core, others], axis=0)
    return (advected + REACT_STEP * change_all) * wet_mask[None]


def reference(ocean, tracers, bottom, stoich):
    current = ocean.reshape(3, NY, NX, LEV)
    tracer_now = tracers.reshape(NTR, NY, NX, LEV)
    wet_mask = (jnp.arange(LEV)[None, None, :] < bottom[:, :, None]).astype(jnp.float32)
    wet_cols = jnp.pad(wet_mask, ((0, 0), (2, 2), (0, 0)))
    wet_rows = jnp.pad(wet_mask, ((2, 2), (0, 0), (0, 0)))
    for step_index in range(STEPS):
        sunlight, heating = optics(tracer_now[2], wet_mask)
        temper = current[2]
        row_margin = jnp.pad(temper, ((1, 1), (0, 0), (0, 0)))
        column_margin = jnp.pad(temper, ((0, 0), (1, 1), (0, 0)))
        current = ocean_update(current, row_margin, column_margin, heating, wet_mask)
        east_wide = jnp.pad(current[0], ((0, 0), (2, 2), (0, 0)))
        north_wide = jnp.pad(current[1], ((2, 2), (0, 0), (0, 0)))

        def advect_one(tracer_field):
            column_change = face_transport(jnp.pad(tracer_field, ((0, 0), (2, 2), (0, 0))), east_wide, wet_cols, 1, NX)
            row_change = face_transport(jnp.pad(tracer_field, ((2, 2), (0, 0), (0, 0))), north_wide, wet_rows, 0, NY)
            return tracer_field - column_change - row_change

        advected = lax.map(advect_one, tracer_now)
        tracer_now = reactions(advected, sunlight, current[2], stoich, wet_mask)
    return current.reshape(ocean.shape), tracer_now.reshape(tracers.shape)
```

```python
import functools

import jax
import jax.numpy as jnp
from jax import lax
from jax.experimental import pallas as pl
from jax.experimental.pallas import tpu as pltpu
from jax.sharding import PartitionSpec as P

LEV = 64
STEPS = 2

ATTEN_WATER = 0.04
ATTEN_CHL = 0.03
PRESSURE = 0.05
TIME_STEP = 0.2
CORIOLIS = 1.0
DAMPING = 0.05
HEAT_GAIN = 2.0
DIFFUSE = 0.2
ADVECT = 0.08
GROWTH = 1.0
HALF_LIGHT = 0.2
HALF_NUTRIENT = 0.5
TEMP_COEF = 0.1
GRAZE = 0.8
HALF_PREY = 0.3
MORTAL = 0.1
REMIN = 0.2
CHL_RELAX = 0.3
CHL_RATIO = 0.5
CHL_GAIN = 0.2
ASSIM = 0.3
GRAZER_LOSS = 0.05
REACT_STEP = 0.2

MESH = pl.DeviceIdType.MESH
HALF = 2 * LEV
CORE = 5
CHUNK = 7
F32 = jnp.float32


def kernel(
    ncomp, nty, ntx,
    tr_in, oc_in, bottom, stoich,
    tr_out, oc_out,
    q0, q1, s0, s1, s2, band,
    rim_q, west_q, east_q, rim_s, west_s, east_s,
    load_sem, send_sem, recv_sem, gsend_sem, grecv_sem,
):
    comp = lax.axis_index("comp")
    ty = lax.axis_index("ty")
    tx = lax.axis_index("tx")
    tile = ty * ncomp + comp
    rows = q0.shape[1]
    ntr = q0.shape[0]
    start = pl.multiple_of(comp * rows, rows)

    load_o = pltpu.make_async_copy(oc_in.at[:, pl.ds(start, rows), :], s0.at[0:3], load_sem.at[0])
    load_q = pltpu.make_async_copy(tr_in.at[:, 0], q0, load_sem.at[1])
    load_o.start()
    load_q.start()

    up = jnp.maximum(tile - 1, 0)
    down = jnp.minimum(tile + 1, ncomp * nty - 1)
    targets = (
        {"comp": lax.rem(down, ncomp), "ty": lax.div(down, ncomp)},
        {"comp": lax.rem(up, ncomp), "ty": lax.div(up, ncomp)},
        {"tx": jnp.minimum(tx + 1, ntx - 1)},
        {"tx": jnp.maximum(tx - 1, 0)},
    )
    has_down, has_up = tile < ncomp * nty - 1, tile > 0
    has_east, has_west = tx < ntx - 1, tx > 0
    sends = (has_down, has_up, has_east, has_west)
    gets = (has_up, has_down, has_west, has_east)

    for ref in (rim_q, west_q, east_q, rim_s, west_s, east_s):
        ref[...] = jnp.zeros(ref.shape, F32)

    barrier = pltpu.get_barrier_semaphore()
    for way in range(4):
        @pl.when(sends[way])
        def _(way=way):
            pl.semaphore_signal(barrier, inc=1, device_id=targets[way], device_id_type=MESH)
    for hop in range(1, ncomp):
        pl.semaphore_signal(
            barrier, inc=1, device_id={"comp": lax.rem(comp + hop, ncomp)}, device_id_type=MESH
        )

    lane = lax.broadcasted_iota(jnp.int32, (rows, HALF), 1)
    sub = lax.broadcasted_iota(jnp.int32, (rows, HALF), 0)
    low = lane < LEV
    level = lax.rem(lane, LEV)
    floor = bottom[pl.ds(start, rows), :]
    wet = [
        (level < jnp.where(low, floor[:, 2 * i : 2 * i + 1], floor[:, 2 * i + 1 : 2 * i + 2])).astype(F32)
        for i in range(2)
    ]
    for i in range(2):
        s0[3, :, i * HALF : (i + 1) * HALF] = wet[i]

    a = lax.broadcasted_iota(jnp.int32, (HALF, HALF), 0)
    b = lax.broadcasted_iota(jnp.int32, (HALF, HALF), 1)
    same = (a < LEV) == (b < LEV)
    incl = jnp.where(same & (a <= b), 1.0, 0.0).astype(jnp.bfloat16)
    excl = jnp.where(same & (a < b), 1.0, 0.0).astype(jnp.bfloat16)

    expect = sum(jnp.where(flag, 1, 0) for flag in sends) + (ncomp - 1)
    pl.semaphore_wait(barrier, expect)

    def exchange(step, kind, state, rim, west, east, count):
        ends = (
            (state.at[0:count, rows - 2 : rows, :], rim.at[step, 0:count, rows - 2 : rows, :]),
            (state.at[0:count, 0:2, :], rim.at[step, 0:count, 0:2, :]),
            (state.at[0:count, :, HALF : 2 * HALF], west.at[step, 0:count]),
            (state.at[0:count, :, 0:HALF], east.at[step, 0:count]),
        )
        return [
            pltpu.make_async_remote_copy(
                src_ref=source,
                dst_ref=target,
                send_sem=send_sem.at[step, kind, way],
                recv_sem=recv_sem.at[step, kind, way],
                device_id=targets[way],
                device_id_type=MESH,
            )
            for way, (source, target) in enumerate(ends)
        ]

    def begin(copies):
        for way in range(4):
            @pl.when(sends[way])
            def _(way=way):
                copies[way].start()

    def arrive(copies):
        for way in range(4):
            @pl.when(gets[way])
            def _(way=way):
                copies[way].wait_recv()

    def left(copies):
        for way in range(4):
            @pl.when(sends[way])
            def _(way=way):
                copies[way].wait_send()

    def level_sums(parts, ladder):
        x = jnp.concatenate(parts, axis=0)
        high = x.astype(jnp.bfloat16)
        rest = x - high.astype(F32)
        mid = rest.astype(jnp.bfloat16)
        last = (rest - mid.astype(F32)).astype(jnp.bfloat16)
        n = x.shape[0]
        y = jnp.dot(
            jnp.concatenate([high, mid, last], axis=0), ladder, preferred_element_type=F32
        )
        y = y[0:n] + y[n : 2 * n] + y[2 * n : 3 * n]
        return [y[i * rows : (i + 1) * rows] for i in range(len(parts))]

    def pick(mask, x, y):
        if x.ndim == 3:
            mask = jnp.broadcast_to(mask[None], x.shape)
        return jnp.where(mask, x, y)

    def swap(x):
        return pltpu.roll(x, LEV, axis=x.ndim - 1)

    def spin(x, shift):
        return pltpu.roll(x, shift, axis=x.ndim - 2)

    first, first_two, final = sub < 1, sub < 2, sub > rows - 2

    def next_row(x, rim):
        return spin(pick(first, rim, x), rows - 1)

    def after_row(x, rim):
        return spin(pick(first_two, rim, x), rows - 2)

    def prev_row(x, rim):
        return spin(pick(final, rim, x), 1)

    def limited(below, middle, above, pos, sign_half, speed, q_a, q_b):
        other = pick(pos, below, above)
        least = jnp.minimum(other, middle)
        most = jnp.maximum(other, middle)
        slope = jnp.maximum(least, 0.0) + jnp.minimum(most, 0.0)
        return speed * (pick(pos, q_a, q_b) + sign_half * slope)

    def halves(ref, *lead):
        return [ref[(*lead, slice(None), slice(0, HALF))], ref[(*lead, slice(None), slice(HALF, 2 * HALF))]]

    copies_s = exchange(0, 0, s0, rim_s, west_s, east_s, 4)
    copies_q = exchange(0, 1, q0, rim_q, west_q, east_q, ntr)
    load_o.wait()
    begin(copies_s)
    load_q.wait()
    begin(copies_q)
    pending = copies_s + copies_q
    pend_s, pend_q = [copies_s], [copies_q]

    states = (s0, s1, s2)
    gathers = []
    wet_ring = None
    for step in range(STEPS):
        q_ref, state, after = (q0, q1)[step], states[step], states[step + 1]
        u, v, temp = (halves(state, k) for k in range(3))
        absorb = [
            (ATTEN_WATER + ATTEN_CHL * jnp.maximum(c, 0.0)) * w
            for c, w in zip(halves(q_ref, 2), wet)
        ]
        above = level_sums(absorb, excl)
        sunlight = [jnp.exp(-x) for x in above]
        heating = [s * (1.0 - jnp.exp(-x)) * w for s, x, w in zip(sunlight, absorb, wet)]

        arrive(copies_s)
        if step == 0:
            wet_line = [west_s[0, 3], *wet, east_s[0, 3]]
            wet_rim = halves(rim_s, 0, 3)
            turned = [swap(x) for x in wet_line]
            col_gate = [
                wet_line[i] * pick(low, turned[i], turned[i + 1]) for i in range(3)
            ]
            row_gate = [w * next_row(w, r) for w, r in zip(wet, wet_rim)]
            rim_gate = [r * spin(w, rows - 1) for w, r in zip(wet, wet_rim)]
        line = [west_s[step, 2], *temp, east_s[step, 2]]
        rim = halves(rim_s, step, 2)
        sums = level_sums(line + rim, incl)
        press, press_rim = sums[:4], sums[4:]
        turned = [swap(x) for x in press]
        u_line = [west_s[step, 0], *u, east_s[step, 0]]
        v_line = [west_s[step, 1], *v, east_s[step, 1]]
        new_u = []
        for i in range(4):
            east = pick(low, turned[i], turned[min(i + 1, 3)])
            west = pick(low, turned[max(i - 1, 0)], turned[i])
            slope = (0.5 * PRESSURE) * (east - west)
            new_u.append(
                wet_line[i] * ((1.0 - DAMPING) * u_line[i] + TIME_STEP * (CORIOLIS * v_line[i] - slope))
            )
        u_rim, v_rim = halves(rim_s, step, 0), halves(rim_s, step, 1)
        new_v, new_v_rim, new_temp = [], [], []
        turned = [swap(x) for x in line]
        for i in range(2):
            slope = (0.5 * PRESSURE) * (
                next_row(press[i + 1], press_rim[i]) - prev_row(press[i + 1], press_rim[i])
            )
            new_v.append(
                wet[i] * ((1.0 - DAMPING) * v[i] - TIME_STEP * (CORIOLIS * u[i] + slope))
            )
            slope = (0.5 * PRESSURE) * (
                next_row(press_rim[i], press[i + 1]) - prev_row(press_rim[i], press[i + 1])
            )
            new_v_rim.append(
                wet_rim[i] * ((1.0 - DAMPING) * v_rim[i] - TIME_STEP * (CORIOLIS * u_rim[i] + slope))
            )
            spread = (
                next_row(temp[i], rim[i])
                + prev_row(temp[i], rim[i])
                + pick(low, turned[i + 1], turned[i + 2])
                + pick(low, turned[i], turned[i + 1])
                - 4.0 * temp[i]
            )
            new_temp.append(
                wet[i] * (temp[i] + TIME_STEP * (HEAT_GAIN * heating[i] + DIFFUSE * spread))
            )
        for i in range(2):
            cols = slice(i * HALF, (i + 1) * HALF)
            after[0, :, cols] = new_u[i + 1]
            after[1, :, cols] = new_v[i]
            after[2, :, cols] = new_temp[i]
        if step + 1 < STEPS:
            copies_s = exchange(step + 1, 0, after, rim_s, west_s, east_s, 3)
            begin(copies_s)
            pend_s.append(copies_s)
        else:
            for hop in range(1, ncomp):
                copy = pltpu.make_async_remote_copy(
                    src_ref=after,
                    dst_ref=band.at[:, pl.ds(start, rows), :],
                    send_sem=gsend_sem.at[hop - 1],
                    recv_sem=grecv_sem.at[hop - 1],
                    device_id={"comp": lax.rem(comp + hop, ncomp)},
                    device_id_type=MESH,
                )
                copy.start()
                gathers.append(copy)
            band[:, pl.ds(start, rows), :] = after[...]

        turned = [swap(x) for x in new_u]
        col_speed = [
            (0.5 * ADVECT) * (new_u[i] + pick(low, turned[i], turned[i + 1])) * col_gate[i]
            for i in range(3)
        ]
        row_speed = [
            (0.5 * ADVECT) * (new_v[i] + next_row(new_v[i], new_v_rim[i])) * row_gate[i]
            for i in range(2)
        ]
        rim_speed = [
            (0.5 * ADVECT) * (new_v_rim[i] + spin(new_v[i], rows - 1)) * rim_gate[i]
            for i in range(2)
        ]

        def gauge(speeds):
            return [(x > 0.0, jnp.where(x > 0.0, 0.5, -0.5), x) for x in speeds]

        col_gauge, row_gauge, rim_gauge = gauge(col_speed), gauge(row_speed), gauge(rim_speed)

        arrive(copies_q)

        def advect(lo, hi):
            part = slice(lo, hi)
            q = [q_ref[part, :, 0:HALF], q_ref[part, :, HALF : 2 * HALF]]
            line = [west_q[step, part], *q, east_q[step, part]]
            rim = [rim_q[step, part, :, 0:HALF], rim_q[step, part, :, HALF : 2 * HALF]]
            turned = [swap(x) for x in line]
            flux = []
            for i in range(3):
                east = pick(low, turned[i], turned[i + 1])
                west = pick(low, turned[max(i - 1, 0)], turned[i])
                here = line[i]
                pos, sign_half, speed = col_gauge[i]
                flux.append(
                    limited(
                        here - west, east - here, line[i + 1] - east,
                        pos, sign_half, speed, here, east,
                    )
                )
            turned = [swap(x) for x in flux]
            out = []
            for i in range(2):
                value = q[i] - (flux[i + 1] - pick(low, turned[i], turned[i + 1]))
                after_one = next_row(q[i], rim[i])
                pos, sign_half, speed = row_gauge[i]
                inner = limited(
                    q[i] - prev_row(q[i], rim[i]), after_one - q[i], after_row(q[i], rim[i]) - after_one,
                    pos, sign_half, speed, q[i], after_one,
                )
                after_one = spin(q[i], rows - 1)
                pos, sign_half, speed = rim_gauge[i]
                outer = limited(
                    rim[i] - spin(rim[i], 1), after_one - rim[i], spin(q[i], rows - 2) - after_one,
                    pos, sign_half, speed, rim[i], after_one,
                )
                out.append(value - (inner - prev_row(inner, outer)))
            return out

        def put(lo, hi, i, value):
            cols = slice(i * HALF, (i + 1) * HALF)
            if step + 1 < STEPS:
                q1[lo:hi, :, cols] = value
            else:
                tr_out[lo:hi, 0, :, cols] = value

        core = advect(0, CORE)
        net = []
        for i in range(2):
            adv = [core[i][k] for k in range(CORE)]
            nutrient, phyto, chloro, grazer, detritus = (jnp.maximum(x, 0.0) for x in adv)
            uptake = (
                GROWTH
                * sunlight[i]
                / (sunlight[i] + HALF_LIGHT)
                * nutrient
                / (nutrient + HALF_NUTRIENT)
                * jnp.exp(TEMP_COEF * new_temp[i])
            )
            growth = uptake * phyto
            grazing = GRAZE * grazer * phyto * phyto / (phyto * phyto + HALF_PREY)
            dying = MORTAL * phyto
            remineral = REMIN * detritus
            changes = (
                remineral - growth,
                growth - grazing - dying,
                CHL_RELAX * (CHL_RATIO * phyto - chloro) + CHL_GAIN * growth,
                ASSIM * grazing - GRAZER_LOSS * grazer,
                dying + (1.0 - ASSIM) * grazing + GRAZER_LOSS * grazer - remineral,
            )
            for k in range(CORE):
                put(k, k + 1, i, ((adv[k] + REACT_STEP * changes[k]) * wet[i])[None])
            net.append(REACT_STEP * (growth - remineral))
        for lo in range(CORE, ntr, CHUNK):
            hi = min(lo + CHUNK, ntr)
            adv = advect(lo, hi)
            for i in range(2):
                for k in range(lo, hi):
                    put(k, k + 1, i, ((adv[i][k - lo] + stoich[k - CORE] * net[i]) * wet[i])[None])
        if step + 1 < STEPS:
            copies_q = exchange(step + 1, 1, q1, rim_q, west_q, east_q, ntr)
            begin(copies_q)
            pend_q.append(copies_q)

    for copies in pend_s + pend_q:
        left(copies)
    for copy in gathers:
        copy.wait()
    oc_out[...] = band[...]


def shards(ocean, tracers, bottom, stoich):
    ncomp, nty, ntx = (lax.axis_size(name) for name in ("comp", "ty", "tx"))
    ntr, _, rows, width = tracers.shape
    vmem = pl.BlockSpec(memory_space=pltpu.VMEM)
    tr_out, oc_out = pl.pallas_call(
        functools.partial(kernel, ncomp, nty, ntx),
        out_shape=(
            jax.ShapeDtypeStruct(tracers.shape, F32),
            jax.ShapeDtypeStruct(ocean.shape, F32),
        ),
        in_specs=[
            pl.BlockSpec(memory_space=pl.ANY),
            pl.BlockSpec(memory_space=pl.ANY),
            vmem,
            pl.BlockSpec(memory_space=pltpu.SMEM),
        ],
        out_specs=(vmem, vmem),
        scratch_shapes=[
            pltpu.VMEM((ntr, rows, width), F32),
            pltpu.VMEM((ntr, rows, width), F32),
            pltpu.VMEM((4, rows, width), F32),
            pltpu.VMEM((3, rows, width), F32),
            pltpu.VMEM((3, rows, width), F32),
            pltpu.VMEM(ocean.shape, F32),
            pltpu.VMEM((STEPS, ntr, rows, width), F32),
            pltpu.VMEM((STEPS, ntr, rows, HALF), F32),
            pltpu.VMEM((STEPS, ntr, rows, HALF), F32),
            pltpu.VMEM((STEPS, 4, rows, width), F32),
            pltpu.VMEM((STEPS, 4, rows, HALF), F32),
            pltpu.VMEM((STEPS, 4, rows, HALF), F32),
            pltpu.SemaphoreType.DMA((2,)),
            pltpu.SemaphoreType.DMA((STEPS, 2, 4)),
            pltpu.SemaphoreType.DMA((STEPS, 2, 4)),
            pltpu.SemaphoreType.DMA((max(ncomp - 1, 1),)),
            pltpu.SemaphoreType.DMA((max(ncomp - 1, 1),)),
        ],
        compiler_params=pltpu.CompilerParams(
            collective_id=0, has_side_effects=True, vmem_limit_bytes=32 * 1024 * 1024
        ),
    )(tracers, ocean, bottom, stoich)
    return oc_out, tr_out


def solution(mesh):
    in_specs = (P(None, "ty", "tx"), P(None, "ty", "comp", "tx"), P("ty", "tx"), P())
    out_specs = (P(None, "ty", "tx"), P(None, "ty", "comp", "tx"))
    return jax.shard_map(shards, mesh=mesh, in_specs=in_specs, out_specs=out_specs, check_vma=False)
```

```python
import functools

import jax
import jax.numpy as jnp
from jax import lax
from jax.experimental import pallas as pl
from jax.experimental.pallas import tpu as pltpu
from jax.sharding import PartitionSpec as P

LEV = 64
STEPS = 2

ATTEN_WATER = 0.04
ATTEN_CHL = 0.03
PRESSURE = 0.05
TIME_STEP = 0.2
CORIOLIS = 1.0
DAMPING = 0.05
HEAT_GAIN = 2.0
DIFFUSE = 0.2
ADVECT = 0.08
GROWTH = 1.0
HALF_LIGHT = 0.2
HALF_NUTRIENT = 0.5
TEMP_COEF = 0.1
GRAZE = 0.8
HALF_PREY = 0.3
MORTAL = 0.1
REMIN = 0.2
CHL_RELAX = 0.3
CHL_RATIO = 0.5
CHL_GAIN = 0.2
ASSIM = 0.3
GRAZER_LOSS = 0.05
REACT_STEP = 0.2

MESH = pl.DeviceIdType.MESH
HALF = 2 * LEV
CORE = 5
CHUNK = 7
F32 = jnp.float32


def kernel(
    ncomp, nty, ntx,
    tr_in, oc_in, bottom_in, stoich_in,
    tr_out, oc_out,
    bottom, stoich, floors, q0, q1, s0, s1, chl, u_all, v_all, wet_all, sun_all,
    rim_q, west_q, east_q, rim_s, west_s, east_s,
    load_sem, send_sem, recv_sem, gsend_sem, grecv_sem,
):
    comp = lax.axis_index("comp")
    ty = lax.axis_index("ty")
    tx = lax.axis_index("tx")
    tile = ty * ncomp + comp
    rows = q0.shape[1]
    ntr = q0.shape[0]
    band = s0.shape[1]
    start = pl.multiple_of(comp * rows, rows)
    mine = pl.ds(start, rows)

    load_o = pltpu.make_async_copy(oc_in, s0.at[0:3], load_sem.at[0])
    load_q = pltpu.make_async_copy(tr_in.at[:, 0], q0, load_sem.at[1])
    load_b = pltpu.make_async_copy(bottom_in, bottom, load_sem.at[2])
    load_c = pltpu.make_async_copy(stoich_in, stoich, load_sem.at[3])
    for load in (load_b, load_o, load_q, load_c):
        load.start()

    up = jnp.maximum(tile - 1, 0)
    down = jnp.minimum(tile + 1, ncomp * nty - 1)
    targets = (
        {"comp": lax.rem(down, ncomp), "ty": lax.div(down, ncomp)},
        {"comp": lax.rem(up, ncomp), "ty": lax.div(up, ncomp)},
        {"tx": jnp.minimum(tx + 1, ntx - 1)},
        {"tx": jnp.maximum(tx - 1, 0)},
    )
    ocean_targets = (
        {"ty": jnp.minimum(ty + 1, nty - 1)},
        {"ty": jnp.maximum(ty - 1, 0)},
        targets[2],
        targets[3],
    )
    peers = [{"comp": lax.rem(comp + hop, ncomp)} for hop in range(1, ncomp)]
    has_down, has_up = tile < ncomp * nty - 1, tile > 0
    has_east, has_west = tx < ntx - 1, tx > 0
    sends = (has_down, has_up, has_east, has_west)
    gets = (has_up, has_down, has_west, has_east)
    has_next, has_last = ty < nty - 1, ty > 0
    ocean_sends = (has_next, has_last, has_east, has_west)
    ocean_gets = (has_last, has_next, has_west, has_east)

    for ref in (rim_q, west_q, east_q, rim_s, west_s, east_s):
        ref[...] = jnp.zeros(ref.shape, F32)

    barrier = pltpu.get_barrier_semaphore()
    for way in range(4):
        @pl.when(sends[way])
        def _(way=way):
            pl.semaphore_signal(barrier, inc=1, device_id=targets[way], device_id_type=MESH)
    for way in range(2):
        @pl.when(ocean_sends[way])
        def _(way=way):
            pl.semaphore_signal(barrier, inc=1, device_id=ocean_targets[way], device_id_type=MESH)
    for peer in peers:
        pl.semaphore_signal(barrier, inc=1, device_id=peer, device_id_type=MESH)

    lane = lax.broadcasted_iota(jnp.int32, (rows, HALF), 1)
    sub = lax.broadcasted_iota(jnp.int32, (rows, HALF), 0)
    low = lane < LEV
    band_lane = lax.broadcasted_iota(jnp.int32, (band, HALF), 1)
    band_sub = lax.broadcasted_iota(jnp.int32, (band, HALF), 0)
    band_low = band_lane < LEV
    level = lax.rem(band_lane, LEV).astype(F32)
    load_b.wait()
    columns = bottom.shape[0]
    spread_of = (
        lax.broadcasted_iota(jnp.int32, (columns, 2 * HALF), 1) // LEV
        == lax.broadcasted_iota(jnp.int32, (columns, 2 * HALF), 0)
    )
    floors[...] = lax.dot_general(
        bottom[...].astype(F32).astype(jnp.bfloat16),
        jnp.where(spread_of, 1.0, 0.0).astype(jnp.bfloat16),
        (((0,), (0,)), ((), ())),
        preferred_element_type=F32,
    )
    wet = []
    for i in range(2):
        floor = floors[:, i * HALF : (i + 1) * HALF]
        wet.append(jnp.where(level < floor, 1.0, 0.0))
        s0[3, :, i * HALF : (i + 1) * HALF] = wet[i]

    a = lax.broadcasted_iota(jnp.int32, (HALF, HALF), 0)
    b = lax.broadcasted_iota(jnp.int32, (HALF, HALF), 1)
    same = (a < LEV) == (b < LEV)
    incl = jnp.where(same & (a <= b), 1.0, 0.0).astype(jnp.bfloat16)
    excl = jnp.where(same & (a < b), 1.0, 0.0).astype(jnp.bfloat16)

    expect = sum(jnp.where(flag, 1, 0) for flag in sends + ocean_sends[:2]) + (ncomp - 1)
    pl.semaphore_wait(barrier, expect)

    def exchange(step, kind, state, rim, west, east, count):
        rows = state.shape[1]
        where = (ocean_targets, targets)[kind]
        ends = (
            (state.at[0:count, rows - 2 : rows, :], rim.at[step, 0:count, rows - 2 : rows, :]),
            (state.at[0:count, 0:2, :], rim.at[step, 0:count, 0:2, :]),
            (state.at[0:count, :, HALF : 2 * HALF], west.at[step, 0:count]),
            (state.at[0:count, :, 0:HALF], east.at[step, 0:count]),
        )
        return [
            pltpu.make_async_remote_copy(
                src_ref=source,
                dst_ref=target,
                send_sem=send_sem.at[step, kind, way],
                recv_sem=recv_sem.at[step, kind, way],
                device_id=where[way],
                device_id_type=MESH,
            )
            for way, (source, target) in enumerate(ends)
        ]

    def begin(copies, sends):
        for way in range(4):
            @pl.when(sends[way])
            def _(way=way):
                copies[way].start()

    def arrive(copies, gets):
        for way in range(4):
            @pl.when(gets[way])
            def _(way=way):
                copies[way].wait_recv()

    def left(copies, sends):
        for way in range(4):
            @pl.when(sends[way])
            def _(way=way):
                copies[way].wait_send()

    def hand_round(step, q_ref):
        copies = [
            pltpu.make_async_remote_copy(
                src_ref=q_ref.at[2],
                dst_ref=chl.at[step, mine, :],
                send_sem=gsend_sem.at[step, k],
                recv_sem=grecv_sem.at[step, k],
                device_id=peer,
                device_id_type=MESH,
            )
            for k, peer in enumerate(peers)
        ]
        for copy in copies:
            copy.start()
        chl[step, mine, :] = q_ref[2]
        return copies

    def level_sums(parts, ladder):
        x = jnp.concatenate(parts, axis=0)
        high = x.astype(jnp.bfloat16)
        rest = x - high.astype(F32)
        mid = rest.astype(jnp.bfloat16)
        last = (rest - mid.astype(F32)).astype(jnp.bfloat16)
        n = x.shape[0]
        y = jnp.dot(
            jnp.concatenate([high, mid, last], axis=0), ladder, preferred_element_type=F32
        )
        y = y[0:n] + y[n : 2 * n] + y[2 * n : 3 * n]
        tall = parts[0].shape[0]
        return [y[i * tall : (i + 1) * tall] for i in range(len(parts))]

    def pick(mask, x, y):
        if x.ndim == 3:
            mask = jnp.broadcast_to(mask[None], x.shape)
        return jnp.where(mask, x, y)

    def swap(x):
        return pltpu.roll(x, LEV, axis=x.ndim - 1)

    def spin(x, shift):
        return pltpu.roll(x, shift, axis=x.ndim - 2)

    def edge(x, count):
        return (sub if x.shape[-2] == rows else band_sub) < count

    def next_row(x, rim):
        return spin(pick(edge(x, 1), rim, x), x.shape[-2] - 1)

    def after_row(x, rim):
        return spin(pick(edge(x, 2), rim, x), x.shape[-2] - 2)

    def prev_row(x, rim):
        return spin(pick(edge(x, x.shape[-2] - 1), x, rim), 1)

    def limited(below, middle, above, pos, sign_half, speed, q_a, q_b):
        other = pick(pos, below, above)
        least = jnp.minimum(other, middle)
        most = jnp.maximum(other, middle)
        slope = jnp.maximum(least, 0.0) + jnp.minimum(most, 0.0)
        return speed * (pick(pos, q_a, q_b) + sign_half * slope)

    def halves(ref, *lead):
        return [ref[(*lead, slice(None), slice(0, HALF))], ref[(*lead, slice(None), slice(HALF, 2 * HALF))]]

    copies_s = exchange(0, 0, s0, rim_s, west_s, east_s, 4)
    copies_q = exchange(0, 1, q0, rim_q, west_q, east_q, ntr)
    load_o.wait()
    begin(copies_s, ocean_sends)
    load_q.wait()
    shared = hand_round(0, q0)
    begin(copies_q, sends)
    pend_s, pend_q, given = [copies_s], [copies_q], [shared]

    def own(ref, lead, offset=0):
        at = pl.ds(start + offset, rows)
        return [ref[(*lead, at, slice(i * HALF, (i + 1) * HALF))] for i in range(ref.shape[-1] // HALF)]

    def lay(ref, values, rims):
        for i in range(2):
            cols = slice(i * HALF, (i + 1) * HALF)
            ref[0:rows, cols] = rims[i][band - rows : band]
            ref[rows : rows + band, cols] = values[i]
            ref[rows + band : 2 * rows + band, cols] = rims[i][0:rows]
        here, before, beyond = own(ref, (), rows), own(ref, ()), own(ref, (), 2 * rows)
        return here, [pick(sub < 1, y, x) for x, y in zip(before, beyond)]

    load_c.wait()
    for step in range(STEPS):
        q_ref, state = (q0, q1)[step], (s0, s1)[step]
        after = s1 if step + 1 < STEPS else oc_out
        u, v, temp = (halves(state, k) for k in range(3))

        arrive(copies_s, ocean_gets)
        if step == 0:
            wet_line = [west_s[0, 3], *wet, east_s[0, 3]]
            wet_rim = halves(rim_s, 0, 3)
            turned = [swap(x) for x in wet_line]
            for i in range(3):
                u_all[:, i * HALF : (i + 1) * HALF] = wet_line[i] * pick(
                    band_low, turned[i], turned[i + 1]
                )
            col_gate = own(u_all, ())[:3]
            wet_own, wet_near = lay(wet_all, wet, wet_rim)
            row_gate = [w * next_row(w, r) for w, r in zip(wet_own, wet_near)]
            rim_gate = [r * spin(w, rows - 1) for w, r in zip(wet_own, wet_near)]
        line = [west_s[step, 2], *temp, east_s[step, 2]]
        rim = halves(rim_s, step, 2)
        sums = level_sums(line + rim, incl)
        press, press_rim = sums[:4], sums[4:]
        turned = [swap(x) for x in press]
        u_line = [west_s[step, 0], *u, east_s[step, 0]]
        v_line = [west_s[step, 1], *v, east_s[step, 1]]
        new_u = []
        for i in range(4):
            east = pick(band_low, turned[i], turned[min(i + 1, 3)])
            west = pick(band_low, turned[max(i - 1, 0)], turned[i])
            slope = (0.5 * PRESSURE) * (east - west)
            new_u.append(
                wet_line[i] * ((1.0 - DAMPING) * u_line[i] + TIME_STEP * (CORIOLIS * v_line[i] - slope))
            )
        u_rim, v_rim = halves(rim_s, step, 0), halves(rim_s, step, 1)
        new_v, new_v_rim, new_temp, spreads = [], [], [], []
        turned = [swap(x) for x in line]
        for i in range(2):
            slope = (0.5 * PRESSURE) * (
                next_row(press[i + 1], press_rim[i]) - prev_row(press[i + 1], press_rim[i])
            )
            new_v.append(
                wet[i] * ((1.0 - DAMPING) * v[i] - TIME_STEP * (CORIOLIS * u[i] + slope))
            )
            slope = (0.5 * PRESSURE) * (
                next_row(press_rim[i], press[i + 1]) - prev_row(press_rim[i], press[i + 1])
            )
            new_v_rim.append(
                wet_rim[i] * ((1.0 - DAMPING) * v_rim[i] - TIME_STEP * (CORIOLIS * u_rim[i] + slope))
            )
            spreads.append(
                next_row(temp[i], rim[i])
                + prev_row(temp[i], rim[i])
                + pick(band_low, turned[i + 1], turned[i + 2])
                + pick(band_low, turned[i], turned[i + 1])
                - 4.0 * temp[i]
            )
        for copy in shared:
            copy.wait_recv()
        absorb = [
            (ATTEN_WATER + ATTEN_CHL * jnp.maximum(c, 0.0)) * w
            for c, w in zip(halves(chl, step), wet)
        ]
        light = [jnp.exp(-x) for x in level_sums(absorb, excl)]
        for i in range(2):
            heating = light[i] * (1.0 - jnp.exp(-absorb[i])) * wet[i]
            new_temp.append(
                wet[i] * (temp[i] + TIME_STEP * (HEAT_GAIN * heating + DIFFUSE * spreads[i]))
            )
        for i in range(2):
            cols = slice(i * HALF, (i + 1) * HALF)
            after[0, :, cols] = new_u[i + 1]
            after[1, :, cols] = new_v[i]
            after[2, :, cols] = new_temp[i]
            sun_all[:, cols] = light[i]
        if step + 1 < STEPS:
            copies_s = exchange(step + 1, 0, after, rim_s, west_s, east_s, 3)
            begin(copies_s, ocean_sends)
            pend_s.append(copies_s)
        for i in range(4):
            u_all[:, i * HALF : (i + 1) * HALF] = new_u[i]
        new_u = own(u_all, ())
        new_v, new_v_rim = lay(v_all, new_v, new_v_rim)
        new_temp, sunlight = own(after, (2,)), own(sun_all, ())

        turned = [swap(x) for x in new_u]
        col_speed = [
            (0.5 * ADVECT) * (new_u[i] + pick(low, turned[i], turned[i + 1])) * col_gate[i]
            for i in range(3)
        ]
        row_speed = [
            (0.5 * ADVECT) * (new_v[i] + next_row(new_v[i], new_v_rim[i])) * row_gate[i]
            for i in range(2)
        ]
        rim_speed = [
            (0.5 * ADVECT) * (new_v_rim[i] + spin(new_v[i], rows - 1)) * rim_gate[i]
            for i in range(2)
        ]

        def gauge(speeds):
            return [(x > 0.0, jnp.where(x > 0.0, 0.5, -0.5), x) for x in speeds]

        col_gauge, row_gauge, rim_gauge = gauge(col_speed), gauge(row_speed), gauge(rim_speed)

        arrive(copies_q, gets)

        def advect(lo, hi):
            part = slice(lo, hi)
            q = [q_ref[part, :, 0:HALF], q_ref[part, :, HALF : 2 * HALF]]
            line = [west_q[step, part], *q, east_q[step, part]]
            rim = [rim_q[step, part, :, 0:HALF], rim_q[step, part, :, HALF : 2 * HALF]]
            turned = [swap(x) for x in line]
            flux = []
            for i in range(3):
                east = pick(low, turned[i], turned[i + 1])
                west = pick(low, turned[max(i - 1, 0)], turned[i])
                here = line[i]
                pos, sign_half, speed = col_gauge[i]
                flux.append(
                    limited(
                        here - west, east - here, line[i + 1] - east,
                        pos, sign_half, speed, here, east,
                    )
                )
            turned = [swap(x) for x in flux]
            out = []
            for i in range(2):
                value = q[i] - (flux[i + 1] - pick(low, turned[i], turned[i + 1]))
                after_one = next_row(q[i], rim[i])
                pos, sign_half, speed = row_gauge[i]
                inner = limited(
                    q[i] - prev_row(q[i], rim[i]), after_one - q[i], after_row(q[i], rim[i]) - after_one,
                    pos, sign_half, speed, q[i], after_one,
                )
                after_one = spin(q[i], rows - 1)
                pos, sign_half, speed = rim_gauge[i]
                outer = limited(
                    rim[i] - spin(rim[i], 1), after_one - rim[i], spin(q[i], rows - 2) - after_one,
                    pos, sign_half, speed, rim[i], after_one,
                )
                out.append(value - (inner - prev_row(inner, outer)))
            return out

        def put(lo, hi, i, value):
            cols = slice(i * HALF, (i + 1) * HALF)
            if step + 1 < STEPS:
                q1[lo:hi, :, cols] = value
            else:
                tr_out[lo:hi, 0, :, cols] = value

        core = advect(0, CORE)
        net = []
        for i in range(2):
            adv = [core[i][k] for k in range(CORE)]
            nutrient, phyto, chloro, grazer, detritus = (jnp.maximum(x, 0.0) for x in adv)
            uptake = (
                GROWTH
                * sunlight[i]
                / (sunlight[i] + HALF_LIGHT)
                * nutrient
                / (nutrient + HALF_NUTRIENT)
                * jnp.exp(TEMP_COEF * new_temp[i])
            )
            growth = uptake * phyto
            grazing = GRAZE * grazer * phyto * phyto / (phyto * phyto + HALF_PREY)
            dying = MORTAL * phyto
            remineral = REMIN * detritus
            changes = (
                remineral - growth,
                growth - grazing - dying,
                CHL_RELAX * (CHL_RATIO * phyto - chloro) + CHL_GAIN * growth,
                ASSIM * grazing - GRAZER_LOSS * grazer,
                dying + (1.0 - ASSIM) * grazing + GRAZER_LOSS * grazer - remineral,
            )
            for k in range(CORE):
                put(k, k + 1, i, ((adv[k] + REACT_STEP * changes[k]) * wet_own[i])[None])
            net.append(REACT_STEP * (growth - remineral))
        if step + 1 < STEPS:
            shared = hand_round(step + 1, q1)
            given.append(shared)
        for lo in range(CORE, ntr, CHUNK):
            hi = min(lo + CHUNK, ntr)
            adv = advect(lo, hi)
            for i in range(2):
                for k in range(lo, hi):
                    put(k, k + 1, i, ((adv[i][k - lo] + stoich[k - CORE] * net[i]) * wet_own[i])[None])
        if step + 1 < STEPS:
            copies_q = exchange(step + 1, 1, q1, rim_q, west_q, east_q, ntr)
            begin(copies_q, sends)
            pend_q.append(copies_q)

    for copies in pend_s:
        left(copies, ocean_sends)
    for copies in pend_q:
        left(copies, sends)
    for copies in given:
        for copy in copies:
            copy.wait_send()


def shards(ocean, tracers, bottom, stoich):
    ncomp, nty, ntx = (lax.axis_size(name) for name in ("comp", "ty", "tx"))
    ntr, _, rows, width = tracers.shape
    band = ocean.shape[1]
    vmem = pl.BlockSpec(memory_space=pltpu.VMEM)
    tr_out, oc_out = pl.pallas_call(
        functools.partial(kernel, ncomp, nty, ntx),
        out_shape=(
            jax.ShapeDtypeStruct(tracers.shape, F32),
            jax.ShapeDtypeStruct(ocean.shape, F32),
        ),
        in_specs=[
            pl.BlockSpec(memory_space=pltpu.HBM),
        ] * 4,
        out_specs=(vmem, vmem),
        scratch_shapes=[
            pltpu.VMEM(bottom.shape[::-1], jnp.int32),
            pltpu.SMEM(stoich.shape, F32),
            pltpu.VMEM((bottom.shape[0], width), F32),
            pltpu.VMEM((ntr, rows, width), F32),
            pltpu.VMEM((ntr, rows, width), F32),
            pltpu.VMEM((4, band, width), F32),
            pltpu.VMEM((3, band, width), F32),
            pltpu.VMEM((STEPS, band, width), F32),
            pltpu.VMEM((band, 2 * width), F32),
            pltpu.VMEM((band + 2 * rows, width), F32),
            pltpu.VMEM((band + 2 * rows, width), F32),
            pltpu.VMEM((band, width), F32),
            pltpu.VMEM((STEPS, ntr, rows, width), F32),
            pltpu.VMEM((STEPS, ntr, rows, HALF), F32),
            pltpu.VMEM((STEPS, ntr, rows, HALF), F32),
            pltpu.VMEM((STEPS, 4, band, width), F32),
            pltpu.VMEM((STEPS, 4, band, HALF), F32),
            pltpu.VMEM((STEPS, 4, band, HALF), F32),
            pltpu.SemaphoreType.DMA((4,)),
            pltpu.SemaphoreType.DMA((STEPS, 2, 4)),
            pltpu.SemaphoreType.DMA((STEPS, 2, 4)),
            pltpu.SemaphoreType.DMA((STEPS, max(ncomp - 1, 1))),
            pltpu.SemaphoreType.DMA((STEPS, max(ncomp - 1, 1))),
        ],
        compiler_params=pltpu.CompilerParams(
            collective_id=0, has_side_effects=True, vmem_limit_bytes=32 * 1024 * 1024
        ),
    )(*(pltpu.with_memory_space_constraint(x, pltpu.HBM) for x in (tracers, ocean, bottom.T, stoich)))
    return oc_out, tr_out


def solution(mesh):
    in_specs = (P(None, "ty", "tx"), P(None, "ty", "comp", "tx"), P("ty", "tx"), P())
    out_specs = (P(None, "ty", "tx"), P(None, "ty", "comp", "tx"))
    return jax.shard_map(shards, mesh=mesh, in_specs=in_specs, out_specs=out_specs, check_vma=False)
```

```python
import functools

import jax
import jax.numpy as jnp
from jax import lax
from jax.experimental import pallas as pl
from jax.experimental.pallas import tpu as pltpu
from jax.sharding import PartitionSpec as P

LEV = 64
STEPS = 2

ATTEN_WATER = 0.04
ATTEN_CHL = 0.03
PRESSURE = 0.05
TIME_STEP = 0.2
CORIOLIS = 1.0
DAMPING = 0.05
HEAT_GAIN = 2.0
DIFFUSE = 0.2
ADVECT = 0.08
GROWTH = 1.0
HALF_LIGHT = 0.2
HALF_NUTRIENT = 0.5
TEMP_COEF = 0.1
GRAZE = 0.8
HALF_PREY = 0.3
MORTAL = 0.1
REMIN = 0.2
CHL_RELAX = 0.3
CHL_RATIO = 0.5
CHL_GAIN = 0.2
ASSIM = 0.3
GRAZER_LOSS = 0.05
REACT_STEP = 0.2

MESH = pl.DeviceIdType.MESH
HALF = 2 * LEV
CORE = 5
CHUNK = 7
F32 = jnp.float32


def kernel(
    ncomp, nty, ntx,
    tr_in, oc_in, bottom_in, stoich_in,
    tr_out, oc_out,
    bottom, stoich, floors, q0, q1, s0, s1, chl, u_all, v_all, wet_all, sun_all,
    rim_q, west_q, east_q, rim_s, west_s, east_s,
    load_sem, send_sem, recv_sem, gsend_sem, grecv_sem,
):
    comp = lax.axis_index("comp")
    ty = lax.axis_index("ty")
    tx = lax.axis_index("tx")
    tile = ty * ncomp + comp
    rows = q0.shape[1]
    ntr = q0.shape[0]
    band = s0.shape[1]
    start = pl.multiple_of(comp * rows, rows)
    mine = pl.ds(start, rows)

    load_o = pltpu.make_async_copy(oc_in, s0.at[0:3], load_sem.at[0])
    load_q = pltpu.make_async_copy(tr_in.at[:, 0], q0, load_sem.at[1])
    load_b = pltpu.make_async_copy(bottom_in, bottom, load_sem.at[2])
    load_c = pltpu.make_async_copy(stoich_in, stoich, load_sem.at[3])
    for load in (load_b, load_o, load_q, load_c):
        load.start()

    up = jnp.maximum(tile - 1, 0)
    down = jnp.minimum(tile + 1, ncomp * nty - 1)
    targets = (
        {"comp": lax.rem(down, ncomp), "ty": lax.div(down, ncomp)},
        {"comp": lax.rem(up, ncomp), "ty": lax.div(up, ncomp)},
        {"tx": jnp.minimum(tx + 1, ntx - 1)},
        {"tx": jnp.maximum(tx - 1, 0)},
    )
    ocean_targets = (
        {"ty": jnp.minimum(ty + 1, nty - 1)},
        {"ty": jnp.maximum(ty - 1, 0)},
        targets[2],
        targets[3],
    )
    peers = [{"comp": lax.rem(comp + hop, ncomp)} for hop in range(1, ncomp)]
    has_down, has_up = tile < ncomp * nty - 1, tile > 0
    has_east, has_west = tx < ntx - 1, tx > 0
    sends = (has_down, has_up, has_east, has_west)
    gets = (has_up, has_down, has_west, has_east)
    has_next, has_last = ty < nty - 1, ty > 0
    ocean_sends = (has_next, has_last, has_east, has_west)
    ocean_gets = (has_last, has_next, has_west, has_east)

    def clear(missing, ref, lo, hi):
        @pl.when(missing)
        def _():
            ref[:, :, lo:hi, :] = jnp.zeros((*ref.shape[:2], hi - lo, ref.shape[3]), F32)

    for ref, above, below in ((rim_q, has_up, has_down), (rim_s, ty > 0, ty < nty - 1)):
        clear(jnp.logical_not(above), ref, ref.shape[2] - 2, ref.shape[2])
        clear(jnp.logical_not(below), ref, 0, 2)
    for ref, there in ((west_q, has_west), (west_s, has_west), (east_q, has_east), (east_s, has_east)):
        clear(jnp.logical_not(there), ref, 0, ref.shape[2])

    barrier = pltpu.get_barrier_semaphore()
    for way in range(4):
        @pl.when(sends[way])
        def _(way=way):
            pl.semaphore_signal(barrier, inc=1, device_id=targets[way], device_id_type=MESH)
    for way in range(2):
        @pl.when(ocean_sends[way])
        def _(way=way):
            pl.semaphore_signal(barrier, inc=1, device_id=ocean_targets[way], device_id_type=MESH)
    for peer in peers:
        pl.semaphore_signal(barrier, inc=1, device_id=peer, device_id_type=MESH)

    for ref in (rim_q, rim_s):
        inside = ref.shape[2] - 4
        ref[:, :, 2 : 2 + inside, :] = jnp.zeros((*ref.shape[:2], inside, ref.shape[3]), F32)

    lane = lax.broadcasted_iota(jnp.int32, (rows, HALF), 1)
    sub = lax.broadcasted_iota(jnp.int32, (rows, HALF), 0)
    low = lane < LEV
    band_lane = lax.broadcasted_iota(jnp.int32, (band, HALF), 1)
    band_sub = lax.broadcasted_iota(jnp.int32, (band, HALF), 0)
    band_low = band_lane < LEV
    level = lax.rem(band_lane, LEV).astype(F32)
    load_b.wait()
    columns = bottom.shape[0]
    spread_of = (
        lax.broadcasted_iota(jnp.int32, (columns, 2 * HALF), 1) // LEV
        == lax.broadcasted_iota(jnp.int32, (columns, 2 * HALF), 0)
    )
    floors[...] = lax.dot_general(
        bottom[...].astype(F32).astype(jnp.bfloat16),
        jnp.where(spread_of, 1.0, 0.0).astype(jnp.bfloat16),
        (((0,), (0,)), ((), ())),
        preferred_element_type=F32,
    )
    wet = []
    for i in range(2):
        floor = floors[:, i * HALF : (i + 1) * HALF]
        wet.append(jnp.where(level < floor, 1.0, 0.0))
        s0[3, :, i * HALF : (i + 1) * HALF] = wet[i]

    a = lax.broadcasted_iota(jnp.int32, (HALF, HALF), 0)
    b = lax.broadcasted_iota(jnp.int32, (HALF, HALF), 1)
    same = (a < LEV) == (b < LEV)
    incl = jnp.where(same & (a <= b), 1.0, 0.0).astype(jnp.bfloat16)
    excl = jnp.where(same & (a < b), 1.0, 0.0).astype(jnp.bfloat16)

    expect = sum(jnp.where(flag, 1, 0) for flag in sends + ocean_sends[:2]) + (ncomp - 1)
    pl.semaphore_wait(barrier, expect)

    def exchange(step, kind, state, rim, west, east, count):
        rows = state.shape[1]
        where = (ocean_targets, targets)[kind]
        ends = (
            (state.at[0:count, rows - 2 : rows, :], rim.at[step, 0:count, rows - 2 : rows, :]),
            (state.at[0:count, 0:2, :], rim.at[step, 0:count, 0:2, :]),
            (state.at[0:count, :, HALF : 2 * HALF], west.at[step, 0:count]),
            (state.at[0:count, :, 0:HALF], east.at[step, 0:count]),
        )
        return [
            pltpu.make_async_remote_copy(
                src_ref=source,
                dst_ref=target,
                send_sem=send_sem.at[step, kind, way],
                recv_sem=recv_sem.at[step, kind, way],
                device_id=where[way],
                device_id_type=MESH,
            )
            for way, (source, target) in enumerate(ends)
        ]

    def begin(copies, sends):
        for way in range(4):
            @pl.when(sends[way])
            def _(way=way):
                copies[way].start()

    def arrive(copies, gets):
        for way in range(4):
            @pl.when(gets[way])
            def _(way=way):
                copies[way].wait_recv()

    def left(copies, sends):
        for way in range(4):
            @pl.when(sends[way])
            def _(way=way):
                copies[way].wait_send()

    def hand_round(step, q_ref):
        copies = [
            pltpu.make_async_remote_copy(
                src_ref=q_ref.at[2],
                dst_ref=chl.at[step, mine, :],
                send_sem=gsend_sem.at[step, k],
                recv_sem=grecv_sem.at[step, k],
                device_id=peer,
                device_id_type=MESH,
            )
            for k, peer in enumerate(peers)
        ]
        for copy in copies:
            copy.start()
        chl[step, mine, :] = q_ref[2]
        return copies

    def level_sums(parts, ladder):
        x = jnp.concatenate(parts, axis=0)
        high = x.astype(jnp.bfloat16)
        rest = x - high.astype(F32)
        mid = rest.astype(jnp.bfloat16)
        last = (rest - mid.astype(F32)).astype(jnp.bfloat16)
        n = x.shape[0]
        y = jnp.dot(
            jnp.concatenate([high, mid, last], axis=0), ladder, preferred_element_type=F32
        )
        y = y[0:n] + y[n : 2 * n] + y[2 * n : 3 * n]
        tall = parts[0].shape[0]
        return [y[i * tall : (i + 1) * tall] for i in range(len(parts))]

    def pick(mask, x, y):
        if x.ndim == 3:
            mask = jnp.broadcast_to(mask[None], x.shape)
        return jnp.where(mask, x, y)

    def swap(x):
        return pltpu.roll(x, LEV, axis=x.ndim - 1)

    def spin(x, shift):
        return pltpu.roll(x, shift, axis=x.ndim - 2)

    def edge(x, count):
        return (sub if x.shape[-2] == rows else band_sub) < count

    def next_row(x, rim):
        return spin(pick(edge(x, 1), rim, x), x.shape[-2] - 1)

    def after_row(x, rim):
        return spin(pick(edge(x, 2), rim, x), x.shape[-2] - 2)

    def prev_row(x, rim):
        return spin(pick(edge(x, x.shape[-2] - 1), x, rim), 1)

    def limited(below, middle, above, pos, sign_half, speed, q_a, q_b):
        other = pick(pos, below, above)
        least = jnp.minimum(other, middle)
        most = jnp.maximum(other, middle)
        slope = jnp.maximum(least, 0.0) + jnp.minimum(most, 0.0)
        return speed * (pick(pos, q_a, q_b) + sign_half * slope)

    def halves(ref, *lead):
        return [ref[(*lead, slice(None), slice(0, HALF))], ref[(*lead, slice(None), slice(HALF, 2 * HALF))]]

    copies_s = exchange(0, 0, s0, rim_s, west_s, east_s, 4)
    copies_q = exchange(0, 1, q0, rim_q, west_q, east_q, ntr)
    load_o.wait()
    begin(copies_s, ocean_sends)
    load_q.wait()
    shared = hand_round(0, q0)
    begin(copies_q, sends)
    pend_s, pend_q, given = [copies_s], [copies_q], [shared]

    def own(ref, lead, offset=0):
        at = pl.ds(start + offset, rows)
        return [ref[(*lead, at, slice(i * HALF, (i + 1) * HALF))] for i in range(ref.shape[-1] // HALF)]

    def lay(ref, values, rims):
        for i in range(2):
            cols = slice(i * HALF, (i + 1) * HALF)
            ref[0:rows, cols] = rims[i][band - rows : band]
            ref[rows : rows + band, cols] = values[i]
            ref[rows + band : 2 * rows + band, cols] = rims[i][0:rows]
        here, before, beyond = own(ref, (), rows), own(ref, ()), own(ref, (), 2 * rows)
        return here, [pick(sub < 1, y, x) for x, y in zip(before, beyond)]

    load_c.wait()
    for step in range(STEPS):
        q_ref, state = (q0, q1)[step], (s0, s1)[step]
        after = s1 if step + 1 < STEPS else oc_out
        u, v, temp = (halves(state, k) for k in range(3))

        arrive(copies_s, ocean_gets)
        if step == 0:
            wet_line = [west_s[0, 3], *wet, east_s[0, 3]]
            wet_rim = halves(rim_s, 0, 3)
            turned = [swap(x) for x in wet_line]
            for i in range(3):
                u_all[:, i * HALF : (i + 1) * HALF] = wet_line[i] * pick(
                    band_low, turned[i], turned[i + 1]
                )
            col_gate = own(u_all, ())[:3]
            wet_own, wet_near = lay(wet_all, wet, wet_rim)
            row_gate = [w * next_row(w, r) for w, r in zip(wet_own, wet_near)]
            rim_gate = [r * spin(w, rows - 1) for w, r in zip(wet_own, wet_near)]
        line = [west_s[step, 2], *temp, east_s[step, 2]]
        rim = halves(rim_s, step, 2)
        sums = level_sums(line + rim, incl)
        press, press_rim = sums[:4], sums[4:]
        turned = [swap(x) for x in press]
        u_line = [west_s[step, 0], *u, east_s[step, 0]]
        v_line = [west_s[step, 1], *v, east_s[step, 1]]
        new_u = []
        for i in range(4):
            east = pick(band_low, turned[i], turned[min(i + 1, 3)])
            west = pick(band_low, turned[max(i - 1, 0)], turned[i])
            slope = (0.5 * PRESSURE) * (east - west)
            new_u.append(
                wet_line[i] * ((1.0 - DAMPING) * u_line[i] + TIME_STEP * (CORIOLIS * v_line[i] - slope))
            )
        u_rim, v_rim = halves(rim_s, step, 0), halves(rim_s, step, 1)
        new_v, new_v_rim, new_temp, spreads = [], [], [], []
        turned = [swap(x) for x in line]
        for i in range(2):
            slope = (0.5 * PRESSURE) * (
                next_row(press[i + 1], press_rim[i]) - prev_row(press[i + 1], press_rim[i])
            )
            new_v.append(
                wet[i] * ((1.0 - DAMPING) * v[i] - TIME_STEP * (CORIOLIS * u[i] + slope))
            )
            slope = (0.5 * PRESSURE) * (
                next_row(press_rim[i], press[i + 1]) - prev_row(press_rim[i], press[i + 1])
            )
            new_v_rim.append(
                wet_rim[i] * ((1.0 - DAMPING) * v_rim[i] - TIME_STEP * (CORIOLIS * u_rim[i] + slope))
            )
            spreads.append(
                next_row(temp[i], rim[i])
                + prev_row(temp[i], rim[i])
                + pick(band_low, turned[i + 1], turned[i + 2])
                + pick(band_low, turned[i], turned[i + 1])
                - 4.0 * temp[i]
            )
        for copy in shared:
            copy.wait_recv()
        absorb = [
            (ATTEN_WATER + ATTEN_CHL * jnp.maximum(c, 0.0)) * w
            for c, w in zip(halves(chl, step), wet)
        ]
        light = [jnp.exp(-x) for x in level_sums(absorb, excl)]
        for i in range(2):
            heating = light[i] * (1.0 - jnp.exp(-absorb[i])) * wet[i]
            new_temp.append(
                wet[i] * (temp[i] + TIME_STEP * (HEAT_GAIN * heating + DIFFUSE * spreads[i]))
            )
        for i in range(2):
            cols = slice(i * HALF, (i + 1) * HALF)
            after[0, :, cols] = new_u[i + 1]
            after[1, :, cols] = new_v[i]
            after[2, :, cols] = new_temp[i]
            sun_all[:, cols] = light[i]
        if step + 1 < STEPS:
            copies_s = exchange(step + 1, 0, after, rim_s, west_s, east_s, 3)
            begin(copies_s, ocean_sends)
            pend_s.append(copies_s)
        for i in range(4):
            u_all[:, i * HALF : (i + 1) * HALF] = new_u[i]
        new_u = own(u_all, ())
        new_v, new_v_rim = lay(v_all, new_v, new_v_rim)
        new_temp, sunlight = own(after, (2,)), own(sun_all, ())

        turned = [swap(x) for x in new_u]
        col_speed = [
            (0.5 * ADVECT) * (new_u[i] + pick(low, turned[i], turned[i + 1])) * col_gate[i]
            for i in range(3)
        ]
        row_speed = [
            (0.5 * ADVECT) * (new_v[i] + next_row(new_v[i], new_v_rim[i])) * row_gate[i]
            for i in range(2)
        ]
        rim_speed = [
            (0.5 * ADVECT) * (new_v_rim[i] + spin(new_v[i], rows - 1)) * rim_gate[i]
            for i in range(2)
        ]

        def gauge(speeds):
            return [(x > 0.0, jnp.where(x > 0.0, 0.5, -0.5), x) for x in speeds]

        col_gauge, row_gauge, rim_gauge = gauge(col_speed), gauge(row_speed), gauge(rim_speed)

        arrive(copies_q, gets)

        def advect(lo, hi):
            part = slice(lo, hi)
            q = [q_ref[part, :, 0:HALF], q_ref[part, :, HALF : 2 * HALF]]
            line = [west_q[step, part], *q, east_q[step, part]]
            rim = [rim_q[step, part, :, 0:HALF], rim_q[step, part, :, HALF : 2 * HALF]]
            turned = [swap(x) for x in line]
            flux = []
            for i in range(3):
                east = pick(low, turned[i], turned[i + 1])
                west = pick(low, turned[max(i - 1, 0)], turned[i])
                here = line[i]
                pos, sign_half, speed = col_gauge[i]
                flux.append(
                    limited(
                        here - west, east - here, line[i + 1] - east,
                        pos, sign_half, speed, here, east,
                    )
                )
            turned = [swap(x) for x in flux]
            out = []
            for i in range(2):
                value = q[i] - (flux[i + 1] - pick(low, turned[i], turned[i + 1]))
                after_one = next_row(q[i], rim[i])
                pos, sign_half, speed = row_gauge[i]
                inner = limited(
                    q[i] - prev_row(q[i], rim[i]), after_one - q[i], after_row(q[i], rim[i]) - after_one,
                    pos, sign_half, speed, q[i], after_one,
                )
                after_one = spin(q[i], rows - 1)
                pos, sign_half, speed = rim_gauge[i]
                outer = limited(
                    rim[i] - spin(rim[i], 1), after_one - rim[i], spin(q[i], rows - 2) - after_one,
                    pos, sign_half, speed, rim[i], after_one,
                )
                out.append(value - (inner - prev_row(inner, outer)))
            return out

        def put(lo, hi, i, value):
            cols = slice(i * HALF, (i + 1) * HALF)
            if step + 1 < STEPS:
                q1[lo:hi, :, cols] = value
            else:
                tr_out[lo:hi, 0, :, cols] = value

        core = advect(0, CORE)
        net = []
        for i in range(2):
            adv = [core[i][k] for k in range(CORE)]
            nutrient, phyto, chloro, grazer, detritus = (jnp.maximum(x, 0.0) for x in adv)
            uptake = (
                GROWTH
                * sunlight[i]
                / (sunlight[i] + HALF_LIGHT)
                * nutrient
                / (nutrient + HALF_NUTRIENT)
                * jnp.exp(TEMP_COEF * new_temp[i])
            )
            growth = uptake * phyto
            grazing = GRAZE * grazer * phyto * phyto / (phyto * phyto + HALF_PREY)
            dying = MORTAL * phyto
            remineral = REMIN * detritus
            changes = (
                remineral - growth,
                growth - grazing - dying,
                CHL_RELAX * (CHL_RATIO * phyto - chloro) + CHL_GAIN * growth,
                ASSIM * grazing - GRAZER_LOSS * grazer,
                dying + (1.0 - ASSIM) * grazing + GRAZER_LOSS * grazer - remineral,
            )
            for k in range(CORE):
                put(k, k + 1, i, ((adv[k] + REACT_STEP * changes[k]) * wet_own[i])[None])
            net.append(REACT_STEP * (growth - remineral))
        if step + 1 < STEPS:
            shared = hand_round(step + 1, q1)
            given.append(shared)
        for lo in range(CORE, ntr, CHUNK):
            hi = min(lo + CHUNK, ntr)
            adv = advect(lo, hi)
            for i in range(2):
                for k in range(lo, hi):
                    put(k, k + 1, i, ((adv[i][k - lo] + stoich[k - CORE] * net[i]) * wet_own[i])[None])
        if step + 1 < STEPS:
            copies_q = exchange(step + 1, 1, q1, rim_q, west_q, east_q, ntr)
            begin(copies_q, sends)
            pend_q.append(copies_q)

    for copies in pend_s:
        left(copies, ocean_sends)
    for copies in pend_q:
        left(copies, sends)
    for copies in given:
        for copy in copies:
            copy.wait_send()


def shards(ocean, tracers, bottom, stoich):
    ncomp, nty, ntx = (lax.axis_size(name) for name in ("comp", "ty", "tx"))
    ntr, _, rows, width = tracers.shape
    band = ocean.shape[1]
    vmem = pl.BlockSpec(memory_space=pltpu.VMEM)
    tr_out, oc_out = pl.pallas_call(
        functools.partial(kernel, ncomp, nty, ntx),
        out_shape=(
            jax.ShapeDtypeStruct(tracers.shape, F32),
            jax.ShapeDtypeStruct(ocean.shape, F32),
        ),
        in_specs=[
            pl.BlockSpec(memory_space=pltpu.HBM),
        ] * 4,
        out_specs=(vmem, vmem),
        scratch_shapes=[
            pltpu.VMEM(bottom.shape[::-1], jnp.int32),
            pltpu.SMEM(stoich.shape, F32),
            pltpu.VMEM((bottom.shape[0], width), F32),
            pltpu.VMEM((ntr, rows, width), F32),
            pltpu.VMEM((ntr, rows, width), F32),
            pltpu.VMEM((4, band, width), F32),
            pltpu.VMEM((3, band, width), F32),
            pltpu.VMEM((STEPS, band, width), F32),
            pltpu.VMEM((band, 2 * width), F32),
            pltpu.VMEM((band + 2 * rows, width), F32),
            pltpu.VMEM((band + 2 * rows, width), F32),
            pltpu.VMEM((band, width), F32),
            pltpu.VMEM((STEPS, ntr, rows, width), F32),
            pltpu.VMEM((STEPS, ntr, rows, HALF), F32),
            pltpu.VMEM((STEPS, ntr, rows, HALF), F32),
            pltpu.VMEM((STEPS, 4, band, width), F32),
            pltpu.VMEM((STEPS, 4, band, HALF), F32),
            pltpu.VMEM((STEPS, 4, band, HALF), F32),
            pltpu.SemaphoreType.DMA((4,)),
            pltpu.SemaphoreType.DMA((STEPS, 2, 4)),
            pltpu.SemaphoreType.DMA((STEPS, 2, 4)),
            pltpu.SemaphoreType.DMA((STEPS, max(ncomp - 1, 1))),
            pltpu.SemaphoreType.DMA((STEPS, max(ncomp - 1, 1))),
        ],
        compiler_params=pltpu.CompilerParams(
            collective_id=0, has_side_effects=True, vmem_limit_bytes=32 * 1024 * 1024
        ),
    )(*(pltpu.with_memory_space_constraint(x, pltpu.HBM) for x in (tracers, ocean, bottom.T, stoich)))
    return oc_out, tr_out


def solution(mesh):
    in_specs = (P(None, "ty", "tx"), P(None, "ty", "comp", "tx"), P("ty", "tx"), P())
    out_specs = (P(None, "ty", "tx"), P(None, "ty", "comp", "tx"))
    return jax.shard_map(shards, mesh=mesh, in_specs=in_specs, out_specs=out_specs, check_vma=False)
```
